128 devices in a mesh: win: 4 (over z_lo, core), rcv: 32 (over x, y, z_hi).
Axes of the slice: x: 4, y: 4, z: 4 (z_hi: 2, z_lo: 2; z = z_hi * 2 + z_lo), core: 2. Of those that a mesh axis runs over, the one named last changes fastest.
Arguments:
- spectra: bfloat16 [32, 2, 1024, 4096], P('win', None, 'rcv'), may hold values from -6 to 6
- sources: bfloat16 [32, 2, 1024, 4096], P('win', None, 'rcv'), may hold values from -6 to 6
- usable: int32 [32, 1024], P('win', 'rcv'), may hold values 0 or 1
- owners: int32 [1], replicated, may hold values from 0 to 31
Outputs:
- correlations: float32 [32, 1024, 768], P('win', 'rcv')
The draws below stay inside these ranges and needn't reach their ends.
All inputs are finite; a program needn't handle non-finite values. No bound on the sum of `usable` on one device may be relied on, other than what follows from the above.
Results may differ from the reference program's by a relative error of at most 0.013.
Values may be sent and summed in bfloat16 or wider, within the bound.
No kernel may reach another device: no remote copies, remote signals or barrier semaphores. Data moves between devices by JAX's collectives and lax.ppermute only.
A program may use at most 256 MiB of HBM per device.

```python
import math
import jax
import jax.numpy as jnp
from jax import lax

F = 4096
LAGS = 768
SRC = 32
WIN_DEV = 8
STEPS = 1
WINDOWS = 32
CHANNELS = 1024
N_WIN = 4
N_RCV = 32


def set_ends(result, rng, least, high):
    shape = result.shape
    spot = [jax.random.randint(jax.random.fold_in(rng, axis), (), 0, shape[axis]) for axis in range(len(shape))]
    result = result.at[tuple(spot)].set(least)
    longest = shape.index(max(shape))
    spot[longest] = (spot[longest] + 1) % shape[longest]
    return result.at[tuple(spot)].set(high)


def level_of(rng, shape, pieces, low, top_value):
    def one(dim, shards_of):
        draws = jax.random.uniform(jax.random.fold_in(jax.random.fold_in(rng, 6), dim), (shards_of,), jnp.float32, low / len(pieces), top_value / len(pieces))
        return jnp.repeat(jnp.exp(draws), shape[dim] // shards_of).reshape((-1,) + (1,) * (len(shape) - dim - 1))

    level = one(*pieces[0])
    for cut in pieces[1:]:
        level = level * one(*cut)
    return level


def bell_draw(rng, shape, width, bound, shards=(), held_as=jnp.bfloat16):
    entries = jax.random.normal(rng, shape, jnp.float32) * width
    if len(shards) > 0:
        entries = level_of(rng, shape, shards, -0.22, 0.18) * entries
    return jnp.clip(entries, min=-bound, max=bound).astype(held_as)


def setup_inputs(seed: int = 0) -> dict:
    seeds = jax.random.split(jax.random.key(seed), 5)
    return {
        "spectra": bell_draw(seeds[0], (WINDOWS, 2, CHANNELS, F), 1.0, 6.0, ((0, 4), (2, 32))),
        "sources": bell_draw(seeds[1], (WINDOWS, 2, CHANNELS, F), 1.0, 6.0, ((0, 4), (2, 32))),
        "usable": set_ends((jax.random.randint(seeds[2], (WINDOWS, CHANNELS), 0, 8) < 7).astype(jnp.int32), jax.random.fold_in(seeds[2], 1), 0, 1),
        "owners": jax.random.randint(seeds[3], (STEPS,), 0, N_RCV).astype(jnp.int32),
    }


def build_table(bins, lags, windows):
    frequency = jnp.arange(bins, dtype=jnp.int32)[:, None]
    lag_index = jnp.arange(lags, dtype=jnp.int32)[None, :] - lags // 2
    period = 2 * bins
    phases = jnp.mod(frequency * lag_index, period).astype(jnp.float32) * (2.0 * math.pi / period)
    weight = jnp.where(frequency == 0, 1.0, 2.0).astype(jnp.float32)
    scaling = 1.0 / math.sqrt(8.0 * bins * windows)
    return jnp.concatenate([weight * jnp.cos(phases), -weight * jnp.sin(phases)], 0) * scaling

def cross_stack(source_part, receivers):
    swapped = jnp.concatenate([receivers[:, 1:2], -receivers[:, 0:1]], 1)
    left = source_part.astype(jnp.float32)
    real_part = jnp.einsum('wcsf,wcrf->srf', left, receivers.astype(jnp.float32))
    imag_part = jnp.einsum('wcsf,wcrf->srf', left, swapped.astype(jnp.float32))
    return jnp.concatenate([real_part, imag_part], -1).astype(jnp.bfloat16)

def reference(spectra, sources, usable, owners):
    flagged = usable.astype(jnp.bfloat16)[:, None, :, None]
    start = owners[0].astype(jnp.int32) * SRC
    chosen = lax.dynamic_slice_in_dim(sources, start, SRC, 2) * lax.dynamic_slice_in_dim(flagged, start, SRC, 2)
    table = build_table(F, LAGS, WIN_DEV * N_WIN)

    def one_block(index):
        offset = (index * SRC).astype(jnp.int32)
        receivers = lax.dynamic_slice_in_dim(spectra, offset, SRC, 2) * lax.dynamic_slice_in_dim(flagged, offset, SRC, 2)
        stacked = jnp.zeros((SRC, SRC, 2 * F), jnp.float32)
        for group in range(N_WIN):
            lower = group * WIN_DEV
            upper = lower + WIN_DEV
            stacked = stacked + cross_stack(chosen[lower:upper], receivers[lower:upper]).astype(jnp.float32)
        lagged = jnp.dot(stacked.reshape(SRC * SRC, 2 * F), table, precision=lax.Precision.HIGHEST, preferred_element_type=jnp.float32)
        return lagged.reshape(SRC, SRC, LAGS)
    blocks = lax.map(one_block, jnp.arange(N_RCV, dtype=jnp.int32))
    return jnp.transpose(blocks, (1, 0, 2, 3)).reshape(SRC, N_RCV * SRC, LAGS)
```

```python
import math

import jax
import jax.numpy as jnp
from jax import lax
from jax.experimental import pallas as pl
from jax.experimental.pallas import tpu as pltpu
from jax.sharding import PartitionSpec as P

LAGS = 768
LANES = 128
CHUNKS = 4
ROWS = 8
MIB = 2**20


def build_table(bins, lags, windows, block):
    low = jnp.arange(64, dtype=jnp.int32)[:, None]
    lag = jnp.arange(lags, dtype=jnp.int32)[None, :] - lags // 2
    period = 2 * bins
    unit = 2.0 * math.pi / period
    angle_low = jnp.mod(low * lag, period).astype(jnp.float32) * unit
    angle_high = jnp.mod(64 * jnp.arange(bins // 64, dtype=jnp.int32)[:, None] * lag, period).astype(jnp.float32) * unit
    scaling = 1.0 / math.sqrt(8.0 * bins * windows)
    cos_low, sin_low = jnp.cos(angle_low)[None], jnp.sin(angle_low)[None]
    cos_high, sin_high = jnp.cos(angle_high)[:, None], jnp.sin(angle_high)[:, None]
    cos_low, sin_low, cos_high, sin_high = lax.optimization_barrier((cos_low, sin_low, cos_high, sin_high))
    bin_index = 64 * jnp.arange(bins // 64, dtype=jnp.int32)[:, None, None] + low[None]
    weight = jnp.where(bin_index == 0, scaling, 2.0 * scaling).astype(jnp.float32)
    real = weight * (cos_high * cos_low - sin_high * sin_low)
    imag = -weight * (sin_high * cos_low + cos_high * sin_low)
    real = real.astype(jnp.bfloat16).reshape(bins // block, block, lags)
    imag = imag.astype(jnp.bfloat16).reshape(bins // block, block, lags)
    return jnp.concatenate([real, imag], 1)


def cut_chunk(sources, flags, place, chunk, per_piece, devices):
    windows, parts, channels, bins = sources.shape
    columns = bins // LANES
    total = devices * per_piece

    def kernel(place_ref, s_ref, f_ref, o_ref, rows):
        w = pl.program_id(0)

        @pl.when(place_ref[1] == 1)
        def _():
            shift = place_ref[0]
            for c in range(parts):
                for column in range(columns):
                    lanes = slice(column * LANES, (column + 1) * LANES)
                    rows[c, column] = s_ref[0, c, :, lanes].astype(jnp.float32) * f_ref[0]
            for c in range(parts):
                for column in range(columns):
                    tile = (w * parts + c) * columns + column
                    spot = lax.rem(tile + shift, total)
                    o_ref[spot] = rows[c, column, pl.ds(chunk, ROWS, stride=CHUNKS)].astype(jnp.bfloat16)

    return pl.pallas_call(
        kernel,
        grid_spec=pltpu.PrefetchScalarGridSpec(
            num_scalar_prefetch=1,
            grid=(windows,),
            in_specs=[
                pl.BlockSpec((1, parts, channels, bins), lambda w, p: (w, 0, 0, 0)),
                pl.BlockSpec((1, channels, LANES), lambda w, p: (w, 0, 0)),
            ],
            out_specs=pl.BlockSpec((total, ROWS, LANES), lambda w, p: (0, 0, 0)),
            scratch_shapes=[pltpu.VMEM((parts, columns, channels, LANES), jnp.float32)],
        ),
        out_shape=jax.ShapeDtypeStruct((total, ROWS, LANES), jnp.bfloat16),
        compiler_params=pltpu.CompilerParams(vmem_limit_bytes=32 * MIB),
        cost_estimate=pl.CostEstimate(flops=2 * sources.size, bytes_accessed=2 * sources.size, transcendentals=0),
    )(place, sources, flags)


def lag_chunk(spectra, flags, tiles, table, place):
    windows, parts, receivers, bins = spectra.shape
    columns = bins // LANES
    total = tiles.shape[0]
    blocks, doubled, lags = table.shape
    block = doubled // 2
    per_block = block // LANES

    def kernel(place_ref, r_ref, f_ref, s_ref, t_ref, o_ref, rf, sf, cross):
        k = pl.program_id(0)
        shift = place_ref[0]

        @pl.when(k == 0)
        def _():
            o_ref[...] = jnp.zeros_like(o_ref)

        for column in range(per_block):
            lanes = slice(column * LANES, (column + 1) * LANES)
            lanes_imag = slice(block + column * LANES, block + (column + 1) * LANES)
            for w in range(windows):
                real = r_ref[w, 0, :, lanes].astype(jnp.float32) * f_ref[w]
                imag = r_ref[w, 1, :, lanes].astype(jnp.float32) * f_ref[w]
                rf[column, w, 0] = real
                rf[column, w, 1] = imag
                rf[column, w, 2] = real + imag
                spots = [
                    lax.rem((w * parts + c) * columns + k * per_block + column + shift, total) for c in range(parts)
                ]
                real = s_ref[spots[0]].astype(jnp.float32)
                imag = s_ref[spots[1]].astype(jnp.float32)
                sf[column, w, 0] = real
                sf[column, w, 1] = imag
                sf[column, w, 2] = real - imag
            for s0 in range(0, ROWS, 4):
                for r0 in range(0, receivers, 16):
                    sums = [[None] * 3 for _ in range(4)]
                    for w in range(windows):
                        right = [rf[column, w, j, r0 : r0 + 16] for j in range(3)]
                        for s in range(4):
                            for j in range(3):
                                left = jnp.broadcast_to(sf[column, w, j, s0 + s : s0 + s + 1], (16, LANES))
                                term = left * right[j]
                                sums[s][j] = term if sums[s][j] is None else sums[s][j] + term
                    for s in range(4):
                        first, second, third = sums[s]
                        row = (s0 + s) * receivers + r0
                        cross[row : row + 16, lanes] = (first + second).astype(jnp.bfloat16)
                        cross[row : row + 16, lanes_imag] = (third - first + second).astype(jnp.bfloat16)
        o_ref[...] += jnp.dot(cross[...], t_ref[0], preferred_element_type=jnp.float32)

    return pl.pallas_call(
        kernel,
        grid_spec=pltpu.PrefetchScalarGridSpec(
            num_scalar_prefetch=1,
            grid=(blocks,),
            in_specs=[
                pl.BlockSpec((windows, parts, receivers, block), lambda k, p: (0, 0, 0, k)),
                pl.BlockSpec((windows, receivers, LANES), lambda k, p: (0, 0, 0)),
                pl.BlockSpec((total, ROWS, LANES), lambda k, p: (0, 0, 0)),
                pl.BlockSpec((1, doubled, lags), lambda k, p: (k, 0, 0)),
            ],
            out_specs=pl.BlockSpec((ROWS * receivers, lags), lambda k, p: (0, 0)),
            scratch_shapes=[
                pltpu.VMEM((per_block, windows, 3, receivers, LANES), jnp.float32),
                pltpu.VMEM((per_block, windows, 3, ROWS, LANES), jnp.float32),
                pltpu.VMEM((ROWS * receivers, doubled), jnp.bfloat16),
            ],
        ),
        out_shape=jax.ShapeDtypeStruct((ROWS * receivers, lags), jnp.float32),
        compiler_params=pltpu.CompilerParams(vmem_limit_bytes=32 * MIB),
        cost_estimate=pl.CostEstimate(
            flops=2 * ROWS * receivers * 2 * bins * lags * 2, bytes_accessed=2 * table.size + 2 * spectra.size, transcendentals=0
        ),
    )(place, spectra, flags, tiles, table)


def reduce_lags(partial, receivers, lags):
    index = lax.axis_index("win")
    high, core = index // 2, index % 2
    partial = partial.reshape(2, 2, 2, receivers, lags)
    kept = lax.dynamic_index_in_dim(partial, core, 1, keepdims=False)
    given = lax.dynamic_index_in_dim(partial, 1 - core, 1, keepdims=False).astype(jnp.bfloat16)
    kept = kept + lax.ppermute(given, "win", [(0, 1), (1, 0), (2, 3), (3, 2)]).astype(jnp.float32)
    given = lax.dynamic_index_in_dim(kept, 1 - high, 0, keepdims=False).astype(jnp.bfloat16)
    kept = lax.dynamic_index_in_dim(kept, high, 0, keepdims=False)
    return kept + lax.ppermute(given, "win", [(0, 2), (2, 0), (1, 3), (3, 1)]).astype(jnp.float32)


def local(spectra, sources, usable, owners):
    windows, parts, channels, bins = spectra.shape
    devices = lax.axis_size("rcv")
    tiles = windows * parts * (bins // LANES)
    per_piece = -(-tiles // (devices - 1))
    owner = owners[0].astype(jnp.int32)
    is_owner = lax.axis_index("rcv") == owner
    place = jnp.stack([per_piece * (owner + 1), is_owner.astype(jnp.int32)])
    flags = jnp.broadcast_to(usable.astype(jnp.float32)[:, :, None], (windows, channels, LANES))
    table = build_table(bins, LAGS, windows * lax.axis_size("win"), 512)

    outputs = []
    piece = None
    for step in range(CHUNKS + 1):
        send = None
        if step < CHUNKS:
            send = cut_chunk(sources, flags, place, step, per_piece, devices)
            send = send.reshape(devices, per_piece, ROWS, LANES)
        if piece is not None:
            spread = jnp.broadcast_to(piece, (devices, per_piece, ROWS, LANES))
            send = spread if send is None else jnp.where(is_owner, send, spread)
        received = lax.all_to_all(send, "rcv", 0, 0)
        piece = lax.dynamic_index_in_dim(received, owner, 0, keepdims=True)
        if step > 0:
            arrived = received.reshape(devices * per_piece, ROWS, LANES)
            partial = lag_chunk(spectra, flags, arrived, table, place)
            outputs.append(reduce_lags(partial, channels, LAGS))
    return jnp.stack(outputs, 1).reshape(2 * CHUNKS, channels, LAGS)


def solution(mesh):
    return jax.shard_map(
        local,
        mesh=mesh,
        in_specs=(P("win", None, "rcv", None), P("win", None, "rcv", None), P("win", "rcv"), P()),
        out_specs=P("win", "rcv", None),
        check_vma=False,
    )
```

```python
import math

import jax
import jax.numpy as jnp
from jax import lax
from jax.experimental import pallas as pl
from jax.experimental.pallas import tpu as pltpu
from jax.sharding import PartitionSpec as P

LAGS = 768
LANES = 128
QUARTERS = 4
WIDE = 256
LIMIT = 8
ROWS = 8
MIB = 2**20


def build_table(bins, lags, windows):
    fine = 64
    low = jnp.arange(fine, dtype=jnp.int32)[:, None]
    high = jnp.arange(bins // fine, dtype=jnp.int32)[:, None] * fine
    lag = jnp.arange(lags, dtype=jnp.int32)[None, :] - lags // 2
    period = 2 * bins
    unit = 2.0 * math.pi / period
    angle_low = jnp.mod(low * lag, period).astype(jnp.float32) * unit
    angle_high = jnp.mod(high * lag, period).astype(jnp.float32) * unit
    scaling = 2.0 / math.sqrt(8.0 * bins * windows)
    tables = (jnp.cos(angle_low) * scaling, jnp.sin(angle_low) * scaling, jnp.cos(angle_high), jnp.sin(angle_high))

    def kernel(cos_low, sin_low, cos_high, sin_high, o_ref):
        def one(h, carry):
            cos_h, sin_h = cos_high[pl.ds(h, 1)], sin_high[pl.ds(h, 1)]
            start = pl.multiple_of(h * fine, fine)
            real = cos_h * cos_low[...] - sin_h * sin_low[...]
            imag = sin_h * cos_low[...] + cos_h * sin_low[...]
            row = lax.broadcasted_iota(jnp.int32, real.shape, 0)
            real = jnp.where(jnp.logical_and(h == 0, row == 0), 0.5 * real, real)
            o_ref[pl.ds(start, fine)] = real.astype(jnp.bfloat16)
            o_ref[pl.ds(bins + start, fine)] = (-imag).astype(jnp.bfloat16)
            return carry

        lax.fori_loop(0, bins // fine, one, 0)

    in_vmem = pl.BlockSpec(memory_space=pltpu.VMEM)
    return pl.pallas_call(
        kernel,
        in_specs=[in_vmem] * 4,
        out_specs=in_vmem,
        out_shape=jax.ShapeDtypeStruct((2 * bins, lags), jnp.bfloat16),
        compiler_params=pltpu.CompilerParams(vmem_limit_bytes=8 * MIB),
        cost_estimate=pl.CostEstimate(flops=16 * bins * lags, bytes_accessed=4 * bins * lags, transcendentals=0),
    )(*tables)


def cut_sources(sources, flags, place):
    windows, parts, channels, bins = sources.shape
    columns = bins // LANES
    wide = columns // QUARTERS
    total = windows * parts * columns

    def kernel(place_ref, s_hbm, f_ref, *refs):
        outs = refs[:QUARTERS]
        held, rows, sems = refs[QUARTERS:]

        @pl.when(place_ref[0] == 1)
        def _():
            def fetch(w):
                return pltpu.make_async_copy(s_hbm.at[w], held.at[w], sems.at[w])

            for w in range(windows):
                fetch(w).start()

            def one(w, carry):
                fetch(w).wait()
                for c in range(parts):
                    for column in range(columns):
                        lanes = slice(column * LANES, (column + 1) * LANES)
                        rows[column] = held[w, c, :, lanes].astype(jnp.float32) * f_ref[w]
                    for d in range(QUARTERS):
                        m = lax.rem(place_ref[1] + d, QUARTERS)
                        for column in range(columns):
                            spot = ((column // wide) * windows * parts + w * parts + c) * wide + column % wide
                            outs[d][spot] = rows[column, pl.ds(m, ROWS, stride=QUARTERS)].astype(jnp.bfloat16)
                return carry

            lax.fori_loop(0, windows, one, 0)

    in_vmem = pl.BlockSpec(memory_space=pltpu.VMEM)
    return pl.pallas_call(
        kernel,
        in_specs=[pl.BlockSpec(memory_space=pltpu.SMEM), pl.BlockSpec(memory_space=pl.ANY), in_vmem],
        out_specs=[in_vmem] * QUARTERS,
        scratch_shapes=[
            pltpu.VMEM(sources.shape, jnp.bfloat16),
            pltpu.VMEM((columns, channels, LANES), jnp.float32),
            pltpu.SemaphoreType.DMA((windows,)),
        ],
        out_shape=[jax.ShapeDtypeStruct((total, ROWS, LANES), jnp.bfloat16)] * QUARTERS,
        compiler_params=pltpu.CompilerParams(vmem_limit_bytes=16 * MIB),
        cost_estimate=pl.CostEstimate(flops=2 * sources.size, bytes_accessed=4 * sources.size, transcendentals=0),
    )(place, sources, flags)


def mask_receivers(spectra, flags):
    windows, parts, receivers, bins = spectra.shape
    columns = bins // LANES

    def kernel(r_ref, f_ref, o_ref):
        def one(column, carry):
            lanes = pl.ds(pl.multiple_of(column * LANES, LANES), LANES)
            for w in range(windows):
                real = r_ref[w, 0, :, lanes].astype(jnp.float32) * f_ref[w]
                imag = r_ref[w, 1, :, lanes].astype(jnp.float32) * f_ref[w]
                o_ref[column, w, 0] = real
                o_ref[column, w, 1] = imag
                o_ref[column, w, 2] = real + imag
            return carry

        lax.fori_loop(0, columns, one, 0)

    in_vmem = pl.BlockSpec(memory_space=pltpu.VMEM)
    return pl.pallas_call(
        kernel,
        in_specs=[in_vmem] * 2,
        out_specs=in_vmem,
        out_shape=jax.ShapeDtypeStruct((columns, windows, 3, receivers, LANES), jnp.float32),
        compiler_params=pltpu.CompilerParams(vmem_limit_bytes=8 * MIB),
        cost_estimate=pl.CostEstimate(flops=4 * spectra.size, bytes_accessed=8 * spectra.size, transcendentals=0),
    )(spectra, flags)


def lag_quarter(receiving, tiles, table, place):
    columns, windows, _, receivers, _ = receiving.shape
    parts = 2
    bins = columns * LANES
    total = tiles.shape[0]
    doubled, lags = table.shape
    wide = columns // QUARTERS
    half = ROWS * receivers // 2

    def kernel(place_ref, r_ref, s_ref, t_ref, kept_ref, given_ref, sf, cross, lagged):
        def one(column, carry):
            near = lax.rem(place_ref[0] + QUARTERS - column // wide, QUARTERS)
            base = near * (total // QUARTERS) + lax.rem(column, wide)
            to_real = pl.ds(pl.multiple_of(column * LANES, LANES), LANES)
            to_imag = pl.ds(pl.multiple_of(bins + column * LANES, LANES), LANES)
            for w in range(windows):
                real = s_ref[base + w * parts * wide].astype(jnp.float32)
                imag = s_ref[base + (w * parts + 1) * wide].astype(jnp.float32)
                sf[w, 0] = real
                sf[w, 1] = imag
                sf[w, 2] = real - imag
            for s0 in range(0, ROWS, 4):
                for r0 in range(0, receivers, 16):
                    sums = [[None] * 3 for _ in range(4)]
                    for w in range(windows):
                        right = [r_ref[column, w, j, r0 : r0 + 16] for j in range(3)]
                        for s in range(4):
                            for j in range(3):
                                left = jnp.broadcast_to(sf[w, j, s0 + s : s0 + s + 1], (16, LANES))
                                term = left * right[j]
                                sums[s][j] = term if sums[s][j] is None else sums[s][j] + term
                    for s in range(4):
                        first, second, third = sums[s]
                        row = (s0 + s) * receivers + r0
                        cross[row : row + 16, to_real] = (first + second).astype(jnp.bfloat16)
                        cross[row : row + 16, to_imag] = (third - first + second).astype(jnp.bfloat16)
            return carry

        lax.fori_loop(0, columns, one, 0)
        for n in range(0, lags, WIDE):
            part = slice(n, n + WIDE)
            lagged[:, part] = jnp.dot(cross[...], t_ref[:, part], preferred_element_type=jnp.float32)
        chip = place_ref[1]
        kept_ref[...] = lagged[pl.ds(pl.multiple_of(chip * half, half), half)]
        given_ref[...] = lagged[pl.ds(pl.multiple_of((1 - chip) * half, half), half)].astype(jnp.bfloat16)

    in_vmem = pl.BlockSpec(memory_space=pltpu.VMEM)
    return pl.pallas_call(
        kernel,
        in_specs=[pl.BlockSpec(memory_space=pltpu.SMEM), in_vmem, in_vmem, in_vmem],
        out_specs=[in_vmem] * 2,
        scratch_shapes=[
            pltpu.VMEM((windows, 3, ROWS, LANES), jnp.float32),
            pltpu.VMEM((2 * half, doubled), jnp.bfloat16),
            pltpu.VMEM((2 * half, lags), jnp.float32),
        ],
        out_shape=[
            jax.ShapeDtypeStruct((half, lags), jnp.float32),
            jax.ShapeDtypeStruct((half, lags), jnp.bfloat16),
        ],
        compiler_params=pltpu.CompilerParams(vmem_limit_bytes=LIMIT * MIB),
        cost_estimate=pl.CostEstimate(
            flops=2 * ROWS * receivers * doubled * lags * 3, bytes_accessed=2 * table.size, transcendentals=0
        ),
    )(place, receiving, tiles, table)


def split_cores(kept, received, place):
    rows, lags = kept[0].shape
    half = rows // 2

    def kernel(place_ref, *refs):
        kept_refs, received_refs = refs[:QUARTERS], refs[QUARTERS : 2 * QUARTERS]
        mine_ref, given_ref = refs[2 * QUARTERS :]
        core = place_ref[1]
        mine = pl.ds(pl.multiple_of(core * half, half), half)
        other = pl.ds(pl.multiple_of((1 - core) * half, half), half)
        for d in range(QUARTERS):
            m = lax.rem(place_ref[0] + QUARTERS - d, QUARTERS)
            mine_ref[m] = kept_refs[d][mine] + received_refs[d][mine].astype(jnp.float32)
            total = kept_refs[d][other] + received_refs[d][other].astype(jnp.float32)
            given_ref[m] = total.astype(jnp.bfloat16)

    in_vmem = pl.BlockSpec(memory_space=pltpu.VMEM)
    return pl.pallas_call(
        kernel,
        in_specs=[pl.BlockSpec(memory_space=pltpu.SMEM)] + [in_vmem] * (2 * QUARTERS),
        out_specs=[in_vmem] * 2,
        out_shape=[
            jax.ShapeDtypeStruct((QUARTERS, half, lags), jnp.float32),
            jax.ShapeDtypeStruct((QUARTERS, half, lags), jnp.bfloat16),
        ],
        compiler_params=pltpu.CompilerParams(vmem_limit_bytes=8 * MIB),
        cost_estimate=pl.CostEstimate(flops=8 * rows * lags, bytes_accessed=32 * rows * lags, transcendentals=0),
    )(place, *kept, *received)


class Grid:
    def __init__(self):
        self.pairs = {}
        side = 4
        for axis in range(2):
            for step in range(1, side):
                moves = []
                for win in range(4):
                    for x in range(side):
                        for y in range(side):
                            for z in range(2):
                                on_x = axis == win % 2
                                nx, ny = ((x + step) % side, y) if on_x else (x, (y + step) % side)
                                moves.append((win * 32 + (x * side + y) * 2 + z, win * 32 + (nx * side + ny) * 2 + z))
                self.pairs[axis, step] = moves

    def move(self, value, axis, step):
        return lax.ppermute(value, ("win", "rcv"), self.pairs[axis, step])

    def flip(self, value):
        return lax.ppermute(value, "rcv", [(i, i ^ 1) for i in range(32)])

    @staticmethod
    def place(index, core):
        x, y = index // 8, (index // 2) % 4
        return jnp.where(core == 0, x, y), jnp.where(core == 0, y, x), index % 2


def pick(values, chosen):
    result = values[0]
    for value, this in zip(values[1:], chosen):
        result = jnp.where(this, value, result)
    return result


def at(value, index):
    return lax.dynamic_index_in_dim(value, index, 0, keepdims=False)


def local(spectra, sources, usable, owners):
    windows, parts, channels, bins = spectra.shape
    grid = Grid()
    steps = range(1, QUARTERS)
    owner = owners[0].astype(jnp.int32)
    win = lax.axis_index("win")
    chip, core = win // 2, win % 2
    rcv = lax.axis_index("rcv")
    u, v, z = grid.place(rcv, core)
    owner_u, owner_v, owner_z = grid.place(owner, core)
    cut_place = jnp.stack([(rcv == owner).astype(jnp.int32), v])
    lag_place = jnp.stack([u, chip])
    end_place = jnp.stack([v, core])
    to_bins = [((u + d) % QUARTERS).astype(jnp.uint32) for d in range(QUARTERS)]
    off_v = [(v - owner_v) % QUARTERS == d for d in steps]
    off_u = [(u - owner_u) % QUARTERS == d for d in steps]
    same_z = z == owner_z
    scalars = (cut_place, lag_place, end_place, to_bins, off_v, off_u, same_z)
    scalars, usable = lax.optimization_barrier((scalars, usable))
    cut_place, lag_place, end_place, to_bins, off_v, off_u, same_z = scalars

    flags = jnp.broadcast_to(usable.astype(jnp.float32)[:, :, None], (windows, channels, LANES))
    table = build_table(bins, LAGS, windows * lax.axis_size("win"))
    receiving = mask_receivers(spectra, flags)
    tiles = windows * parts * (bins // LANES)
    cut = cut_sources(sources, flags, cut_place)
    cut = [part.reshape(QUARTERS, tiles // QUARTERS, ROWS, LANES) for part in cut]
    dealt = [cut[0]] + [grid.move(cut[d], 1, d) for d in steps]
    mine = pick(dealt, off_v)
    mine, table, receiving = lax.optimization_barrier((mine, table, receiving))
    dealt = [at(mine, to_bins[0])] + [grid.move(at(mine, to_bins[d]), 0, d) for d in steps]
    mine = pick(dealt, off_u)
    mine = jnp.where(same_z, mine, grid.flip(mine))
    row = jnp.stack([mine] + [grid.move(mine, 0, d) for d in steps])
    quarters = [row] + [grid.move(row, 1, d) for d in steps]

    kept, received = [None] * QUARTERS, [None] * QUARTERS
    for d in (0, 1, 3, 2):
        kept[d], given = lag_quarter(receiving, quarters[d].reshape(tiles, ROWS, LANES), table, lag_place)
        received[d] = lax.ppermute(given, "win", [(0, 2), (2, 0), (1, 3), (3, 1)])
    kept, given = split_cores(kept, received, end_place)
    result = kept + lax.ppermute(given, "win", [(0, 1), (1, 0), (2, 3), (3, 2)]).astype(jnp.float32)
    return result.reshape(QUARTERS, 2, channels, LAGS).transpose(1, 0, 2, 3).reshape(2 * QUARTERS, channels, LAGS)


def solution(mesh):
    return jax.shard_map(
        local,
        mesh=mesh,
        in_specs=(P("win", None, "rcv", None), P("win", None, "rcv", None), P("win", "rcv"), P()),
        out_specs=P("win", "rcv", None),
        check_vma=False,
    )
```

```python
import math

import jax
import jax.numpy as jnp
from jax import lax
from jax.experimental import pallas as pl
from jax.experimental.pallas import tpu as pltpu
from jax.sharding import PartitionSpec as P

LAGS = 768
LANES = 128
QUARTERS = 4
WIDE = 256
LIMIT = 16
GROUPS = ((0,), (1, 3), (2,))
ROWS = 8
MIB = 2**20


def build_table(bins, lags, windows):
    fine = 64
    low = jnp.arange(fine, dtype=jnp.int32)[:, None]
    high = jnp.arange(bins // fine, dtype=jnp.int32)[:, None] * fine
    lag = jnp.arange(lags, dtype=jnp.int32)[None, :] - lags // 2
    period = 2 * bins
    unit = 2.0 * math.pi / period
    angle_low = jnp.mod(low * lag, period).astype(jnp.float32) * unit
    angle_high = jnp.mod(high * lag, period).astype(jnp.float32) * unit
    scaling = 2.0 / math.sqrt(8.0 * bins * windows)
    tables = (jnp.cos(angle_low) * scaling, jnp.sin(angle_low) * scaling, jnp.cos(angle_high), jnp.sin(angle_high))

    def kernel(cos_low, sin_low, cos_high, sin_high, o_ref):
        def one(h, carry):
            cos_h, sin_h = cos_high[pl.ds(h, 1)], sin_high[pl.ds(h, 1)]
            start = pl.multiple_of(h * fine, fine)
            real = cos_h * cos_low[...] - sin_h * sin_low[...]
            imag = sin_h * cos_low[...] + cos_h * sin_low[...]
            row = lax.broadcasted_iota(jnp.int32, real.shape, 0)
            real = jnp.where(jnp.logical_and(h == 0, row == 0), 0.5 * real, real)
            o_ref[pl.ds(start, fine)] = real.astype(jnp.bfloat16)
            o_ref[pl.ds(bins + start, fine)] = (-imag).astype(jnp.bfloat16)
            return carry

        lax.fori_loop(0, bins // fine, one, 0)

    in_vmem = pl.BlockSpec(memory_space=pltpu.VMEM)
    return pl.pallas_call(
        kernel,
        in_specs=[in_vmem] * 4,
        out_specs=in_vmem,
        out_shape=jax.ShapeDtypeStruct((2 * bins, lags), jnp.bfloat16),
        compiler_params=pltpu.CompilerParams(vmem_limit_bytes=8 * MIB),
        cost_estimate=pl.CostEstimate(flops=16 * bins * lags, bytes_accessed=4 * bins * lags, transcendentals=0),
    )(*tables)


def cut_sources(sources, flags, place):
    windows, parts, channels, bins = sources.shape
    columns = bins // LANES
    wide = columns // QUARTERS
    total = windows * parts * columns

    def kernel(place_ref, s_hbm, f_ref, *refs):
        outs = refs[:QUARTERS]
        held, rows, sems = refs[QUARTERS:]

        @pl.when(place_ref[0] == 1)
        def _():
            def fetch(w):
                return pltpu.make_async_copy(s_hbm.at[w], held.at[w], sems.at[w])

            for w in range(windows):
                fetch(w).start()

            def one(w, carry):
                fetch(w).wait()
                for c in range(parts):
                    for column in range(columns):
                        lanes = slice(column * LANES, (column + 1) * LANES)
                        rows[column] = held[w, c, :, lanes].astype(jnp.float32) * f_ref[w]
                    for d in range(QUARTERS):
                        m = lax.rem(place_ref[1] + d, QUARTERS)
                        for column in range(columns):
                            spot = ((column // wide) * windows * parts + w * parts + c) * wide + column % wide
                            outs[d][spot] = rows[column, pl.ds(m, ROWS, stride=QUARTERS)].astype(jnp.bfloat16)
                return carry

            lax.fori_loop(0, windows, one, 0)

    in_vmem = pl.BlockSpec(memory_space=pltpu.VMEM)
    return pl.pallas_call(
        kernel,
        in_specs=[pl.BlockSpec(memory_space=pltpu.SMEM), pl.BlockSpec(memory_space=pl.ANY), in_vmem],
        out_specs=[in_vmem] * QUARTERS,
        scratch_shapes=[
            pltpu.VMEM(sources.shape, jnp.bfloat16),
            pltpu.VMEM((columns, channels, LANES), jnp.float32),
            pltpu.SemaphoreType.DMA((windows,)),
        ],
        out_shape=[jax.ShapeDtypeStruct((total, ROWS, LANES), jnp.bfloat16)] * QUARTERS,
        compiler_params=pltpu.CompilerParams(vmem_limit_bytes=16 * MIB),
        cost_estimate=pl.CostEstimate(flops=2 * sources.size, bytes_accessed=4 * sources.size, transcendentals=0),
    )(place, sources, flags)


def mask_receivers(spectra, flags):
    windows, parts, receivers, bins = spectra.shape
    columns = bins // LANES

    def kernel(r_ref, f_ref, o_ref):
        def one(column, carry):
            lanes = pl.ds(pl.multiple_of(column * LANES, LANES), LANES)
            for w in range(windows):
                real = r_ref[w, 0, :, lanes].astype(jnp.float32) * f_ref[w]
                imag = r_ref[w, 1, :, lanes].astype(jnp.float32) * f_ref[w]
                o_ref[column, w, 0] = real
                o_ref[column, w, 1] = imag
                o_ref[column, w, 2] = real + imag
            return carry

        lax.fori_loop(0, columns, one, 0)

    in_vmem = pl.BlockSpec(memory_space=pltpu.VMEM)
    return pl.pallas_call(
        kernel,
        in_specs=[in_vmem] * 2,
        out_specs=in_vmem,
        out_shape=jax.ShapeDtypeStruct((columns, windows, 3, receivers, LANES), jnp.float32),
        compiler_params=pltpu.CompilerParams(vmem_limit_bytes=8 * MIB),
        cost_estimate=pl.CostEstimate(flops=4 * spectra.size, bytes_accessed=8 * spectra.size, transcendentals=0),
    )(spectra, flags)


def lag_quarters(receiving, tiles, table, place, side=None):
    columns, windows, _, receivers, _ = receiving.shape
    parts = 2
    bins = columns * LANES
    total = tiles[0].shape[0]
    number = len(tiles)
    doubled, lags = table.shape
    wide = columns // QUARTERS
    half = ROWS * receivers // 2

    sides = (0, 1) if side is None else (side,)
    shapes = [
        jax.ShapeDtypeStruct((number * half, lags), jnp.float32),
        jax.ShapeDtypeStruct((number * half, lags), jnp.bfloat16),
    ]

    def kernel(place_ref, r_ref, t_ref, *refs):
        outs = refs[number : number + len(sides)]
        sf, cross = refs[number + len(sides) :]
        chip = place_ref[1]

        def one(column, carry):
            near = lax.rem(place_ref[0] + QUARTERS - column // wide, QUARTERS)
            base = near * (total // QUARTERS) + lax.rem(column, wide)
            to_real = pl.ds(pl.multiple_of(column * LANES, LANES), LANES)
            to_imag = pl.ds(pl.multiple_of(bins + column * LANES, LANES), LANES)
            for q in range(number):
                for w in range(windows):
                    real = refs[q][base + w * parts * wide].astype(jnp.float32)
                    imag = refs[q][base + (w * parts + 1) * wide].astype(jnp.float32)
                    if side is not None:
                        first = chip == side
                        real = jnp.where(first, real[:4], real[4:])
                        imag = jnp.where(first, imag[:4], imag[4:])
                    sf[q, w, 0] = real
                    sf[q, w, 1] = imag
                    sf[q, w, 2] = real - imag
                for s0 in range(0, 4 * len(sides), 4):
                    for r0 in range(0, receivers, 16):
                        sums = [[None] * 3 for _ in range(4)]
                        for w in range(windows):
                            right = [r_ref[column, w, j, r0 : r0 + 16] for j in range(3)]
                            for s in range(4):
                                for j in range(3):
                                    left = jnp.broadcast_to(sf[q, w, j, s0 + s : s0 + s + 1], (16, LANES))
                                    term = left * right[j]
                                    sums[s][j] = term if sums[s][j] is None else sums[s][j] + term
                        for s in range(4):
                            first, second, third = sums[s]
                            turn = lax.rem(chip + s0 // 4, 2) * number * half + q * half if side is None else q * half
                            row = pl.ds(pl.multiple_of(turn + s * receivers + r0, 16), 16)
                            cross[row, to_real] = (first + second).astype(jnp.bfloat16)
                            cross[row, to_imag] = (third - first + second).astype(jnp.bfloat16)
            return carry

        lax.fori_loop(0, columns, one, 0)
        for n in range(0, lags, WIDE):
            part = slice(n, n + WIDE)
            value = jnp.dot(cross[...], t_ref[:, part], preferred_element_type=jnp.float32)
            for i, out in enumerate(outs):
                out[:, part] = value[i * number * half : (i + 1) * number * half].astype(out.dtype)

    in_vmem = pl.BlockSpec(memory_space=pltpu.VMEM)
    return pl.pallas_call(
        kernel,
        in_specs=[pl.BlockSpec(memory_space=pltpu.SMEM)] + [in_vmem] * (2 + number),
        out_specs=[in_vmem] * len(sides),
        scratch_shapes=[
            pltpu.VMEM((number, windows, 3, 4 * len(sides), LANES), jnp.float32),
            pltpu.VMEM((len(sides) * number * half, doubled), jnp.bfloat16),
        ],
        out_shape=[shapes[i] for i in sides],
        compiler_params=pltpu.CompilerParams(vmem_limit_bytes=LIMIT * MIB),
        cost_estimate=pl.CostEstimate(
            flops=len(sides) * number * half * 2 * doubled * lags * 3, bytes_accessed=2 * table.size, transcendentals=0
        ),
    )(place, receiving, table, *tiles)


def split_cores(kept, received, groups, place):
    rows, lags = kept[0].shape
    rows = rows // len(groups[0])
    half = rows // 2
    count = len(groups)

    def kernel(place_ref, *refs):
        kept_refs, received_refs = refs[:count], refs[count : 2 * count]
        mine_ref, given_ref = refs[2 * count :]
        core = place_ref[1]
        for group, kept_ref, received_ref in zip(groups, kept_refs, received_refs):
            for i, d in enumerate(group):
                mine = pl.ds(pl.multiple_of(i * rows + core * half, half), half)
                other = pl.ds(pl.multiple_of(i * rows + (1 - core) * half, half), half)
                m = lax.rem(place_ref[0] + QUARTERS - d, QUARTERS)
                mine_ref[m] = kept_ref[mine] + received_ref[mine].astype(jnp.float32)
                total = kept_ref[other] + received_ref[other].astype(jnp.float32)
                given_ref[m] = total.astype(jnp.bfloat16)

    in_vmem = pl.BlockSpec(memory_space=pltpu.VMEM)
    return pl.pallas_call(
        kernel,
        in_specs=[pl.BlockSpec(memory_space=pltpu.SMEM)] + [in_vmem] * (2 * count),
        out_specs=[in_vmem] * 2,
        out_shape=[
            jax.ShapeDtypeStruct((QUARTERS, half, lags), jnp.float32),
            jax.ShapeDtypeStruct((QUARTERS, half, lags), jnp.bfloat16),
        ],
        compiler_params=pltpu.CompilerParams(vmem_limit_bytes=8 * MIB),
        cost_estimate=pl.CostEstimate(flops=8 * rows * lags, bytes_accessed=32 * rows * lags, transcendentals=0),
    )(place, *kept, *received)


class Grid:
    def __init__(self):
        self.pairs = {}
        side = 4
        for axis in range(2):
            for step in range(1, side):
                moves = []
                for win in range(4):
                    for x in range(side):
                        for y in range(side):
                            for z in range(2):
                                on_x = axis == win % 2
                                nx, ny = ((x + step) % side, y) if on_x else (x, (y + step) % side)
                                moves.append((win * 32 + (x * side + y) * 2 + z, win * 32 + (nx * side + ny) * 2 + z))
                self.pairs[axis, step] = moves

    def move(self, value, axis, step):
        return lax.ppermute(value, ("win", "rcv"), self.pairs[axis, step])

    def flip(self, value):
        return lax.ppermute(value, "rcv", [(i, i ^ 1) for i in range(32)])

    @staticmethod
    def place(index, core):
        x, y = index // 8, (index // 2) % 4
        return jnp.where(core == 0, x, y), jnp.where(core == 0, y, x), index % 2


def pick(values, chosen):
    result = values[0]
    for value, this in zip(values[1:], chosen):
        result = jnp.where(this, value, result)
    return result


def at(value, index):
    return lax.dynamic_index_in_dim(value, index, 0, keepdims=False)


def local(spectra, sources, usable, owners):
    windows, parts, channels, bins = spectra.shape
    grid = Grid()
    steps = range(1, QUARTERS)
    owner = owners[0].astype(jnp.int32)
    win = lax.axis_index("win")
    chip, core = win // 2, win % 2
    rcv = lax.axis_index("rcv")
    u, v, z = grid.place(rcv, core)
    owner_u, owner_v, owner_z = grid.place(owner, core)
    cut_place = jnp.stack([(rcv == owner).astype(jnp.int32), v])
    lag_place = jnp.stack([u, chip])
    end_place = jnp.stack([v, core])
    to_bins = [((u + d) % QUARTERS).astype(jnp.uint32) for d in range(QUARTERS)]
    off_v = [(v - owner_v) % QUARTERS == d for d in steps]
    off_u = [(u - owner_u) % QUARTERS == d for d in steps]
    same_z = z == owner_z
    scalars = (cut_place, lag_place, end_place, to_bins, off_v, off_u, same_z)
    scalars, usable = lax.optimization_barrier((scalars, usable))
    cut_place, lag_place, end_place, to_bins, off_v, off_u, same_z = scalars

    flags = jnp.broadcast_to(usable.astype(jnp.float32)[:, :, None], (windows, channels, LANES))
    table = build_table(bins, LAGS, windows * lax.axis_size("win"))
    receiving = mask_receivers(spectra, flags)
    tiles = windows * parts * (bins // LANES)
    cut = cut_sources(sources, flags, cut_place)
    cut = [part.reshape(QUARTERS, tiles // QUARTERS, ROWS, LANES) for part in cut]
    dealt = [cut[0]] + [grid.move(cut[d], 1, d) for d in steps]
    mine = pick(dealt, off_v)
    mine, table, receiving = lax.optimization_barrier((mine, table, receiving))
    dealt = [at(mine, to_bins[0])] + [grid.move(at(mine, to_bins[d]), 0, d) for d in steps]
    mine = pick(dealt, off_u)
    mine = jnp.where(same_z, mine, grid.flip(mine))
    row = jnp.stack([mine] + [grid.move(mine, 0, d) for d in steps])
    quarters = [row, grid.move(row, 1, 1), None, grid.move(row, 1, 3)]

    kept, received = [], []
    for group in GROUPS:
        if group == GROUPS[1]:
            row, quarters[1], quarters[3] = lax.optimization_barrier((row, quarters[1], quarters[3]))
            quarters[2] = grid.move(row, 1, 2)
        blocks = [quarters[d].reshape(tiles, ROWS, LANES) for d in group]
        if group != GROUPS[-1]:
            mine, given = lag_quarters(receiving, blocks, table, lag_place)
        else:
            (given,) = lag_quarters(receiving, blocks, table, lag_place, 1)
            given, lag_place = lax.optimization_barrier((given, lag_place))
            (mine,) = lag_quarters(receiving, blocks, table, lag_place, 0)
        mine, lag_place = lax.optimization_barrier((mine, lag_place))
        kept.append(mine)
        received.append(lax.ppermute(given, "win", [(0, 2), (2, 0), (1, 3), (3, 1)]))
    kept, given = split_cores(kept, received, GROUPS, end_place)
    result = kept + lax.ppermute(given, "win", [(0, 1), (1, 0), (2, 3), (3, 2)]).astype(jnp.float32)
    return result.reshape(QUARTERS, 2, channels, LAGS).transpose(1, 0, 2, 3).reshape(2 * QUARTERS, channels, LAGS)


def solution(mesh):
    return jax.shard_map(
        local,
        mesh=mesh,
        in_specs=(P("win", None, "rcv", None), P("win", None, "rcv", None), P("win", "rcv"), P()),
        out_specs=P("win", "rcv", None),
        check_vma=False,
    )
```

```python
import math

import jax
import jax.numpy as jnp
from jax import lax
from jax.experimental import pallas as pl
from jax.experimental.pallas import tpu as pltpu
from jax.sharding import PartitionSpec as P

LAGS = 768
LANES = 128
QUARTERS = 4
WIDE = 256
LIMIT = 16
GROUPS = ((0,), (1, 3), (2,))
ROWS = 8
MIB = 2**20


def build_table(bins, lags, windows):
    fine = 64
    low = jnp.arange(fine, dtype=jnp.int32)[:, None]
    high = jnp.arange(bins // fine, dtype=jnp.int32)[:, None] * fine
    lag = jnp.arange(lags, dtype=jnp.int32)[None, :] - lags // 2
    period = 2 * bins
    unit = 2.0 * math.pi / period
    angle_low = jnp.mod(low * lag, period).astype(jnp.float32) * unit
    angle_high = jnp.mod(high * lag, period).astype(jnp.float32) * unit
    scaling = 2.0 / math.sqrt(8.0 * bins * windows)
    tables = (jnp.cos(angle_low) * scaling, jnp.sin(angle_low) * scaling, jnp.cos(angle_high), jnp.sin(angle_high))

    def kernel(cos_low, sin_low, cos_high, sin_high, o_ref):
        def one(h, carry):
            cos_h, sin_h = cos_high[pl.ds(h, 1)], sin_high[pl.ds(h, 1)]
            start = pl.multiple_of(h * fine, fine)
            real = cos_h * cos_low[...] - sin_h * sin_low[...]
            imag = sin_h * cos_low[...] + cos_h * sin_low[...]
            row = lax.broadcasted_iota(jnp.int32, real.shape, 0)
            real = jnp.where(jnp.logical_and(h == 0, row == 0), 0.5 * real, real)
            o_ref[pl.ds(start, fine)] = real.astype(jnp.bfloat16)
            o_ref[pl.ds(bins + start, fine)] = (-imag).astype(jnp.bfloat16)
            return carry

        lax.fori_loop(0, bins // fine, one, 0)

    in_vmem = pl.BlockSpec(memory_space=pltpu.VMEM)
    return pl.pallas_call(
        kernel,
        in_specs=[in_vmem] * 4,
        out_specs=in_vmem,
        out_shape=jax.ShapeDtypeStruct((2 * bins, lags), jnp.bfloat16),
        compiler_params=pltpu.CompilerParams(vmem_limit_bytes=8 * MIB),
        cost_estimate=pl.CostEstimate(flops=16 * bins * lags, bytes_accessed=4 * bins * lags, transcendentals=0),
    )(*tables)


def cut_sources(sources, flags, place, wanted):
    windows, parts, channels, bins = sources.shape
    columns = bins // LANES
    wide = columns // QUARTERS
    total = windows * parts * columns

    def kernel(place_ref, s_ref, f_ref, *refs):
        outs, rows = refs[:-1], refs[-1]

        @pl.when(place_ref[0] == 1)
        def _():
            def one(w, carry):
                for c in range(parts):
                    for column in range(columns):
                        lanes = slice(column * LANES, (column + 1) * LANES)
                        rows[c, column] = s_ref[w, c, :, lanes].astype(jnp.float32) * f_ref[w]
                    for d, out in zip(wanted, outs):
                        m = lax.rem(place_ref[1] + d, QUARTERS)
                        for column in range(columns):
                            spot = ((column // wide) * windows * parts + w * parts + c) * wide + column % wide
                            out[spot] = rows[c, column, pl.ds(m, ROWS, stride=QUARTERS)].astype(jnp.bfloat16)
                return carry

            lax.fori_loop(0, windows, one, 0)

    in_vmem = pl.BlockSpec(memory_space=pltpu.VMEM)
    return pl.pallas_call(
        kernel,
        in_specs=[pl.BlockSpec(memory_space=pltpu.SMEM), in_vmem, in_vmem],
        out_specs=[in_vmem] * len(wanted),
        scratch_shapes=[pltpu.VMEM((parts, columns, channels, LANES), jnp.float32)],
        out_shape=[jax.ShapeDtypeStruct((total, ROWS, LANES), jnp.bfloat16)] * len(wanted),
        compiler_params=pltpu.CompilerParams(vmem_limit_bytes=8 * MIB),
        cost_estimate=pl.CostEstimate(flops=2 * sources.size, bytes_accessed=4 * sources.size, transcendentals=0),
    )(place, sources, flags)


def mask_receivers(spectra, flags):
    windows, parts, receivers, bins = spectra.shape
    columns = bins // LANES

    def kernel(r_ref, f_ref, o_ref):
        def one(column, carry):
            lanes = pl.ds(pl.multiple_of(column * LANES, LANES), LANES)
            for w in range(windows):
                real = r_ref[w, 0, :, lanes].astype(jnp.float32) * f_ref[w]
                imag = r_ref[w, 1, :, lanes].astype(jnp.float32) * f_ref[w]
                o_ref[column, w, 0] = real
                o_ref[column, w, 1] = imag
                o_ref[column, w, 2] = real + imag
            return carry

        lax.fori_loop(0, columns, one, 0)

    in_vmem = pl.BlockSpec(memory_space=pltpu.VMEM)
    return pl.pallas_call(
        kernel,
        in_specs=[in_vmem] * 2,
        out_specs=in_vmem,
        out_shape=jax.ShapeDtypeStruct((columns, windows, 3, receivers, LANES), jnp.float32),
        compiler_params=pltpu.CompilerParams(vmem_limit_bytes=8 * MIB),
        cost_estimate=pl.CostEstimate(flops=4 * spectra.size, bytes_accessed=8 * spectra.size, transcendentals=0),
    )(spectra, flags)


def lag_quarters(receiving, tiles, table, place, side=None, nears=None, before=None):
    columns, windows, _, receivers, _ = receiving.shape
    parts = 2
    bins = columns * LANES
    number = len(tiles)
    doubled, lags = table.shape
    wide = columns // QUARTERS
    half = ROWS * receivers // 2
    piece = windows * parts * wide
    count = columns if nears is None else wide * len(nears)
    added = 0 if before is None else 1

    sides = (0, 1) if side is None else (side,)
    shapes = [
        jax.ShapeDtypeStruct((number * half, lags), jnp.float32),
        jax.ShapeDtypeStruct((number * half, lags), jnp.bfloat16),
    ]
    outputs = [shapes[i] for i in sides]
    if nears is not None and before is None:
        outputs = [jax.ShapeDtypeStruct((2 * number * half, lags), jnp.float32)]

    def kernel(place_ref, r_ref, t_ref, *refs):
        outs = refs[number + added : number + added + len(outputs)]
        sf, cross = refs[number + added + len(outputs) :]
        chip = place_ref[1]

        def one(i, carry):
            if nears is None:
                column = i
                near = lax.rem(place_ref[0] + QUARTERS - column // wide, QUARTERS)
                base = near * piece + lax.rem(column, wide)
                real_column, imag_column = column, columns + column
            else:
                turn = i // wide
                quarter = lax.rem(place_ref[0] + QUARTERS - nears[0] - turn, QUARTERS)
                column = quarter * wide + lax.rem(i, wide)
                base = (nears[0] + turn) * piece + lax.rem(i, wide)
                real_column = turn * 2 * wide + lax.rem(i, wide)
                imag_column = real_column + wide
            to_real = pl.ds(pl.multiple_of(real_column * LANES, LANES), LANES)
            to_imag = pl.ds(pl.multiple_of(imag_column * LANES, LANES), LANES)
            for q in range(number):
                for w in range(windows):
                    real = refs[q][base + w * parts * wide].astype(jnp.float32)
                    imag = refs[q][base + (w * parts + 1) * wide].astype(jnp.float32)
                    if side is not None:
                        first = chip == side
                        real = jnp.where(first, real[:4], real[4:])
                        imag = jnp.where(first, imag[:4], imag[4:])
                    sf[q, w, 0] = real
                    sf[q, w, 1] = imag
                    sf[q, w, 2] = real - imag
                for s0 in range(0, 4 * len(sides), 4):
                    for r0 in range(0, receivers, 16):
                        sums = [[None] * 3 for _ in range(4)]
                        for w in range(windows):
                            right = [r_ref[column, w, j, r0 : r0 + 16] for j in range(3)]
                            for s in range(4):
                                for j in range(3):
                                    left = jnp.broadcast_to(sf[q, w, j, s0 + s : s0 + s + 1], (16, LANES))
                                    term = left * right[j]
                                    sums[s][j] = term if sums[s][j] is None else sums[s][j] + term
                        for s in range(4):
                            first, second, third = sums[s]
                            turn = lax.rem(chip + s0 // 4, 2) * number * half + q * half if side is None else q * half
                            row = pl.ds(pl.multiple_of(turn + s * receivers + r0, 16), 16)
                            cross[row, to_real] = (first + second).astype(jnp.bfloat16)
                            cross[row, to_imag] = (third - first + second).astype(jnp.bfloat16)
            return carry

        lax.fori_loop(0, count, one, 0)
        for n in range(0, lags, WIDE):
            part = slice(n, n + WIDE)
            if nears is None:
                value = jnp.dot(cross[...], t_ref[:, part], preferred_element_type=jnp.float32)
            else:
                value = None if before is None else refs[number][:, part]
                span = wide * LANES
                for j in range(2 * len(nears)):
                    quarter = lax.rem(place_ref[0] + QUARTERS - nears[j // 2], QUARTERS)
                    some = pl.ds(pl.multiple_of(j % 2 * bins + quarter * span, span), span)
                    term = jnp.dot(
                        cross[:, j * span : (j + 1) * span], t_ref[some, part], preferred_element_type=jnp.float32
                    )
                    value = term if value is None else value + term
            for i, out in enumerate(outs):
                rows = number * half if len(outs) == len(sides) else 2 * number * half
                out[:, part] = value[i * rows : (i + 1) * rows].astype(out.dtype)

    in_vmem = pl.BlockSpec(memory_space=pltpu.VMEM)
    return pl.pallas_call(
        kernel,
        in_specs=[pl.BlockSpec(memory_space=pltpu.SMEM)] + [in_vmem] * (2 + number + added),
        out_specs=[in_vmem] * len(outputs),
        scratch_shapes=[
            pltpu.VMEM((number, windows, 3, 4 * len(sides), LANES), jnp.float32),
            pltpu.VMEM((len(sides) * number * half, 2 * count * LANES), jnp.bfloat16),
        ],
        out_shape=outputs,
        compiler_params=pltpu.CompilerParams(vmem_limit_bytes=LIMIT * MIB),
        cost_estimate=pl.CostEstimate(
            flops=len(sides) * number * half * 4 * count * LANES * lags * 3, bytes_accessed=2 * table.size, transcendentals=0
        ),
    )(place, receiving, table, *tiles, *([before] if added else []))


def split_cores(kept, received, groups, place):
    rows, lags = kept[0].shape
    rows = rows // len(groups[0])
    half = rows // 2
    count = len(groups)

    def kernel(place_ref, *refs):
        kept_refs, received_refs = refs[:count], refs[count : 2 * count]
        mine_ref, given_ref = refs[2 * count :]
        core = place_ref[1]
        for group, kept_ref, received_ref in zip(groups, kept_refs, received_refs):
            for i, d in enumerate(group):
                mine = pl.ds(pl.multiple_of(i * rows + core * half, half), half)
                other = pl.ds(pl.multiple_of(i * rows + (1 - core) * half, half), half)
                m = lax.rem(place_ref[0] + QUARTERS - d, QUARTERS)
                mine_ref[m] = kept_ref[mine] + received_ref[mine].astype(jnp.float32)
                total = kept_ref[other] + received_ref[other].astype(jnp.float32)
                given_ref[m] = total.astype(jnp.bfloat16)

    in_vmem = pl.BlockSpec(memory_space=pltpu.VMEM)
    return pl.pallas_call(
        kernel,
        in_specs=[pl.BlockSpec(memory_space=pltpu.SMEM)] + [in_vmem] * (2 * count),
        out_specs=[in_vmem] * 2,
        out_shape=[
            jax.ShapeDtypeStruct((QUARTERS, half, lags), jnp.float32),
            jax.ShapeDtypeStruct((QUARTERS, half, lags), jnp.bfloat16),
        ],
        compiler_params=pltpu.CompilerParams(vmem_limit_bytes=8 * MIB),
        cost_estimate=pl.CostEstimate(flops=8 * rows * lags, bytes_accessed=32 * rows * lags, transcendentals=0),
    )(place, *kept, *received)


class Grid:
    def __init__(self):
        self.pairs = {}
        side = 4
        for axis in range(2):
            for step in range(1, side):
                moves = []
                for win in range(4):
                    for x in range(side):
                        for y in range(side):
                            for z in range(2):
                                on_x = axis == win % 2
                                nx, ny = ((x + step) % side, y) if on_x else (x, (y + step) % side)
                                moves.append((win * 32 + (x * side + y) * 2 + z, win * 32 + (nx * side + ny) * 2 + z))
                self.pairs[axis, step] = moves

    def move(self, value, axis, step):
        return lax.ppermute(value, ("win", "rcv"), self.pairs[axis, step])

    def flip(self, value):
        return lax.ppermute(value, "rcv", [(i, i ^ 1) for i in range(32)])

    @staticmethod
    def place(index, core):
        x, y = index >> 3, (index >> 1) & 3
        return jnp.where(core == 0, x, y), jnp.where(core == 0, y, x), index & 1


def pick(values, chosen):
    result = values[0]
    for value, this in zip(values[1:], chosen):
        result = jnp.where(this, value, result)
    return result


def at(value, index):
    return lax.dynamic_index_in_dim(value, index, 0, keepdims=False)


def local(spectra, sources, usable, owners):
    windows, parts, channels, bins = spectra.shape
    grid = Grid()
    steps = range(1, QUARTERS)
    owner = owners[0].astype(jnp.int32)
    win = lax.axis_index("win")
    chip, core = win >> 1, win & 1
    rcv = lax.axis_index("rcv")
    u, v, z = grid.place(rcv, core)
    owner_u, owner_v, owner_z = grid.place(owner, core)
    cut_place = jnp.stack([(rcv == owner).astype(jnp.int32), v])
    lag_place = jnp.stack([u, chip])
    end_place = jnp.stack([v, core])
    to_bins = [((u + d) & 3).astype(jnp.uint32) for d in range(QUARTERS)]
    off_v = [(v - owner_v) & 3 == d for d in steps]
    off_u = [(u - owner_u) & 3 == d for d in steps]
    same_z = z == owner_z
    scalars = (cut_place, lag_place, end_place, to_bins, off_v, off_u, same_z)
    scalars, usable = lax.optimization_barrier((scalars, usable))
    cut_place, lag_place, end_place, to_bins, off_v, off_u, same_z = scalars

    flags = jnp.broadcast_to(usable.astype(jnp.float32)[:, :, None], (windows, channels, LANES))
    table = build_table(bins, LAGS, windows * lax.axis_size("win"))
    receiving = mask_receivers(spectra, flags)
    tiles = windows * parts * (bins // LANES)
    cut = cut_sources(sources, flags, cut_place, (1, 2, 3))
    own = cut_sources(sources, flags, cut_place, (0,))
    cut = own + cut
    cut = [part.reshape(QUARTERS, tiles // QUARTERS, ROWS, LANES) for part in cut]
    dealt = [cut[0]] + [grid.move(cut[d], 1, d) for d in steps]
    mine = pick(dealt, off_v)
    mine, table, receiving = lax.optimization_barrier((mine, table, receiving))
    dealt = [at(mine, to_bins[0])] + [grid.move(at(mine, to_bins[d]), 0, d) for d in steps]
    mine = pick(dealt, off_u)
    mine = jnp.where(same_z, mine, grid.flip(mine))
    near = [mine] + [grid.move(mine, 0, d) for d in steps]
    (early,) = lag_quarters(receiving, [mine], table, lag_place, nears=(0,))
    near, early = lax.optimization_barrier((near, early))
    row = jnp.stack(near)
    quarters = [row, grid.move(row, 1, 1), None, grid.move(row, 1, 3)]

    kept, received = [], []
    for group in GROUPS:
        if group == GROUPS[1]:
            row, quarters[1], quarters[3] = lax.optimization_barrier((row, quarters[1], quarters[3]))
            quarters[2] = grid.move(row, 1, 2)
        blocks = [quarters[d].reshape(tiles, ROWS, LANES) for d in group]
        if group == GROUPS[0]:
            mine, given = lag_quarters(receiving, blocks, table, lag_place, nears=(1, 2, 3), before=early)
        elif group != GROUPS[-1]:
            mine, given = lag_quarters(receiving, blocks, table, lag_place)
        else:
            (given,) = lag_quarters(receiving, blocks, table, lag_place, 1)
            given, lag_place = lax.optimization_barrier((given, lag_place))
            (mine,) = lag_quarters(receiving, blocks, table, lag_place, 0)
        mine, lag_place = lax.optimization_barrier((mine, lag_place))
        kept.append(mine)
        received.append(lax.ppermute(given, "win", [(0, 2), (2, 0), (1, 3), (3, 1)]))
    kept, given = split_cores(kept, received, GROUPS, end_place)
    result = kept + lax.ppermute(given, "win", [(0, 1), (1, 0), (2, 3), (3, 2)]).astype(jnp.float32)
    return result.reshape(QUARTERS, 2, channels, LAGS).transpose(1, 0, 2, 3).reshape(2 * QUARTERS, channels, LAGS)


def solution(mesh):
    return jax.shard_map(
        local,
        mesh=mesh,
        in_specs=(P("win", None, "rcv", None), P("win", None, "rcv", None), P("win", "rcv"), P()),
        out_specs=P("win", "rcv", None),
        check_vma=False,
    )
```

```python
import math

import jax
import jax.numpy as jnp
from jax import lax
from jax.experimental import pallas as pl
from jax.experimental.pallas import tpu as pltpu
from jax.sharding import PartitionSpec as P

LAGS = 768
LANES = 128
QUARTERS = 4
WIDE = 256
LIMIT = 16
GROUPS = ((0,), (1, 3), (2,))
ROWS = 8
MIB = 2**20


def build_table(bins, lags, windows):
    fine = 64
    low = jnp.arange(fine, dtype=jnp.int32)[:, None]
    high = jnp.arange(bins // fine, dtype=jnp.int32)[:, None] * fine
    lag = jnp.arange(lags, dtype=jnp.int32)[None, :] - lags // 2
    period = 2 * bins
    unit = 2.0 * math.pi / period
    angle_low = jnp.mod(low * lag, period).astype(jnp.float32) * unit
    angle_high = jnp.mod(high * lag, period).astype(jnp.float32) * unit
    scaling = 2.0 / math.sqrt(8.0 * bins * windows)
    tables = (jnp.cos(angle_low) * scaling, jnp.sin(angle_low) * scaling, jnp.cos(angle_high), jnp.sin(angle_high))

    def kernel(cos_low, sin_low, cos_high, sin_high, o_ref):
        def one(h, carry):
            cos_h, sin_h = cos_high[pl.ds(h, 1)], sin_high[pl.ds(h, 1)]
            start = pl.multiple_of(h * fine, fine)
            real = cos_h * cos_low[...] - sin_h * sin_low[...]
            imag = sin_h * cos_low[...] + cos_h * sin_low[...]
            row = lax.broadcasted_iota(jnp.int32, real.shape, 0)
            real = jnp.where(jnp.logical_and(h == 0, row == 0), 0.5 * real, real)
            o_ref[pl.ds(start, fine)] = real.astype(jnp.bfloat16)
            o_ref[pl.ds(bins + start, fine)] = (-imag).astype(jnp.bfloat16)
            return carry

        lax.fori_loop(0, bins // fine, one, 0)

    in_vmem = pl.BlockSpec(memory_space=pltpu.VMEM)
    return pl.pallas_call(
        kernel,
        in_specs=[in_vmem] * 4,
        out_specs=in_vmem,
        out_shape=jax.ShapeDtypeStruct((2 * bins, lags), jnp.bfloat16),
        compiler_params=pltpu.CompilerParams(vmem_limit_bytes=8 * MIB),
        cost_estimate=pl.CostEstimate(flops=16 * bins * lags, bytes_accessed=4 * bins * lags, transcendentals=0),
    )(*tables)


def cut_sources(sources, flags, place, wanted):
    windows, parts, channels, bins = sources.shape
    columns = bins // LANES
    wide = columns // QUARTERS
    total = windows * parts * columns

    def kernel(place_ref, s_ref, f_ref, *refs):
        outs, rows = refs[:-1], refs[-1]

        @pl.when(place_ref[0] == 1)
        def _():
            def one(w, carry):
                for c in range(parts):
                    for column in range(columns):
                        lanes = slice(column * LANES, (column + 1) * LANES)
                        rows[c, column] = s_ref[w, c, :, lanes].astype(jnp.float32) * f_ref[w]
                    for d, out in zip(wanted, outs):
                        m = lax.rem(place_ref[1] + d, QUARTERS)
                        for column in range(columns):
                            spot = ((column // wide) * windows * parts + w * parts + c) * wide + column % wide
                            out[spot] = rows[c, column, pl.ds(m, ROWS, stride=QUARTERS)].astype(jnp.bfloat16)
                return carry

            lax.fori_loop(0, windows, one, 0)

    in_vmem = pl.BlockSpec(memory_space=pltpu.VMEM)
    return pl.pallas_call(
        kernel,
        in_specs=[pl.BlockSpec(memory_space=pltpu.SMEM), in_vmem, in_vmem],
        out_specs=[in_vmem] * len(wanted),
        scratch_shapes=[pltpu.VMEM((parts, columns, channels, LANES), jnp.float32)],
        out_shape=[jax.ShapeDtypeStruct((total, ROWS, LANES), jnp.bfloat16)] * len(wanted),
        compiler_params=pltpu.CompilerParams(vmem_limit_bytes=8 * MIB),
        cost_estimate=pl.CostEstimate(flops=2 * sources.size, bytes_accessed=4 * sources.size, transcendentals=0),
    )(place, sources, flags)


def mask_receivers(spectra, flags):
    windows, parts, receivers, bins = spectra.shape
    columns = bins // LANES

    def kernel(r_ref, f_ref, o_ref):
        def one(column, carry):
            lanes = pl.ds(pl.multiple_of(column * LANES, LANES), LANES)
            for w in range(windows):
                real = r_ref[w, 0, :, lanes].astype(jnp.float32) * f_ref[w]
                imag = r_ref[w, 1, :, lanes].astype(jnp.float32) * f_ref[w]
                o_ref[column, w, 0] = real
                o_ref[column, w, 1] = imag
                o_ref[column, w, 2] = real + imag
            return carry

        lax.fori_loop(0, columns, one, 0)

    in_vmem = pl.BlockSpec(memory_space=pltpu.VMEM)
    return pl.pallas_call(
        kernel,
        in_specs=[in_vmem] * 2,
        out_specs=in_vmem,
        out_shape=jax.ShapeDtypeStruct((columns, windows, 3, receivers, LANES), jnp.float32),
        compiler_params=pltpu.CompilerParams(vmem_limit_bytes=8 * MIB),
        cost_estimate=pl.CostEstimate(flops=4 * spectra.size, bytes_accessed=8 * spectra.size, transcendentals=0),
    )(spectra, flags)


def lag_quarters(receiving, tiles, table, place, side=None, nears=None, before=None, held=0):
    columns, windows, _, receivers, _ = receiving.shape
    parts = 2
    bins = columns * LANES
    number = len(tiles)
    doubled, lags = table.shape
    wide = columns // QUARTERS
    half = ROWS * receivers // 2
    piece = windows * parts * wide
    count = columns if nears is None else wide * len(nears)
    added = 0 if before is None else 1

    sides = (0, 1) if side is None else (side,)
    shapes = [
        jax.ShapeDtypeStruct((number * half, lags), jnp.float32),
        jax.ShapeDtypeStruct((number * half, lags), jnp.bfloat16),
    ]
    outputs = [shapes[i] for i in sides]
    if nears is not None and before is None:
        outputs = [jax.ShapeDtypeStruct((2 * number * half, lags), jnp.float32)]

    def kernel(place_ref, r_ref, t_ref, *refs):
        outs = refs[number + added : number + added + len(outputs)]
        sf, cross = refs[number + added + len(outputs) :]
        chip = place_ref[1]

        def one(i, carry):
            if nears is None:
                column = i
                near = lax.rem(place_ref[0] + QUARTERS - column // wide, QUARTERS)
                base = near * piece + lax.rem(column, wide)
                real_column, imag_column = column, columns + column
            else:
                turn = i // wide
                quarter = lax.rem(place_ref[0] + QUARTERS - nears[0] - turn, QUARTERS)
                column = quarter * wide + lax.rem(i, wide)
                base = (nears[0] - held + turn) * piece + lax.rem(i, wide)
                real_column = turn * 2 * wide + lax.rem(i, wide)
                imag_column = real_column + wide
            to_real = pl.ds(pl.multiple_of(real_column * LANES, LANES), LANES)
            to_imag = pl.ds(pl.multiple_of(imag_column * LANES, LANES), LANES)
            for q in range(number):
                for w in range(windows):
                    real = refs[q][base + w * parts * wide].astype(jnp.float32)
                    imag = refs[q][base + (w * parts + 1) * wide].astype(jnp.float32)
                    if side is not None:
                        first = chip == side
                        real = jnp.where(first, real[:4], real[4:])
                        imag = jnp.where(first, imag[:4], imag[4:])
                    sf[q, w, 0] = real
                    sf[q, w, 1] = imag
                    sf[q, w, 2] = real - imag
                for s0 in range(0, 4 * len(sides), 4):
                    for r0 in range(0, receivers, 16):
                        sums = [[None] * 3 for _ in range(4)]
                        for w in range(windows):
                            right = [r_ref[column, w, j, r0 : r0 + 16] for j in range(3)]
                            for s in range(4):
                                for j in range(3):
                                    left = jnp.broadcast_to(sf[q, w, j, s0 + s : s0 + s + 1], (16, LANES))
                                    term = left * right[j]
                                    sums[s][j] = term if sums[s][j] is None else sums[s][j] + term
                        for s in range(4):
                            first, second, third = sums[s]
                            turn = lax.rem(chip + s0 // 4, 2) * number * half + q * half if side is None else q * half
                            row = pl.ds(pl.multiple_of(turn + s * receivers + r0, 16), 16)
                            cross[row, to_real] = (first + second).astype(jnp.bfloat16)
                            cross[row, to_imag] = (third - first + second).astype(jnp.bfloat16)
            return carry

        lax.fori_loop(0, count, one, 0)
        for n in range(0, lags, WIDE):
            part = slice(n, n + WIDE)
            if nears is None:
                value = jnp.dot(cross[...], t_ref[:, part], preferred_element_type=jnp.float32)
            else:
                value = None if before is None else refs[number][:, part]
                span = wide * LANES
                for j in range(2 * len(nears)):
                    quarter = lax.rem(place_ref[0] + QUARTERS - nears[j // 2], QUARTERS)
                    some = pl.ds(pl.multiple_of(j % 2 * bins + quarter * span, span), span)
                    term = jnp.dot(
                        cross[:, j * span : (j + 1) * span], t_ref[some, part], preferred_element_type=jnp.float32
                    )
                    value = term if value is None else value + term
            for i, out in enumerate(outs):
                rows = number * half if len(outs) == len(sides) else 2 * number * half
                out[:, part] = value[i * rows : (i + 1) * rows].astype(out.dtype)

    in_vmem = pl.BlockSpec(memory_space=pltpu.VMEM)
    return pl.pallas_call(
        kernel,
        in_specs=[pl.BlockSpec(memory_space=pltpu.SMEM)] + [in_vmem] * (2 + number + added),
        out_specs=[in_vmem] * len(outputs),
        scratch_shapes=[
            pltpu.VMEM((number, windows, 3, 4 * len(sides), LANES), jnp.float32),
            pltpu.VMEM((len(sides) * number * half, 2 * count * LANES), jnp.bfloat16),
        ],
        out_shape=outputs,
        compiler_params=pltpu.CompilerParams(vmem_limit_bytes=LIMIT * MIB),
        cost_estimate=pl.CostEstimate(
            flops=len(sides) * number * half * 4 * count * LANES * lags * 3, bytes_accessed=2 * table.size, transcendentals=0
        ),
    )(place, receiving, table, *tiles, *([before] if added else []))


def split_cores(kept, received, groups, place):
    rows, lags = kept[0].shape
    rows = rows // len(groups[0])
    half = rows // 2
    count = len(groups)

    def kernel(place_ref, *refs):
        kept_refs, received_refs = refs[:count], refs[count : 2 * count]
        mine_ref, given_ref = refs[2 * count :]
        core = place_ref[1]
        for group, kept_ref, received_ref in zip(groups, kept_refs, received_refs):
            for i, d in enumerate(group):
                mine = pl.ds(pl.multiple_of(i * rows + core * half, half), half)
                other = pl.ds(pl.multiple_of(i * rows + (1 - core) * half, half), half)
                m = lax.rem(place_ref[0] + QUARTERS - d, QUARTERS)
                mine_ref[m] = kept_ref[mine] + received_ref[mine].astype(jnp.float32)
                total = kept_ref[other] + received_ref[other].astype(jnp.float32)
                given_ref[m] = total.astype(jnp.bfloat16)

    in_vmem = pl.BlockSpec(memory_space=pltpu.VMEM)
    return pl.pallas_call(
        kernel,
        in_specs=[pl.BlockSpec(memory_space=pltpu.SMEM)] + [in_vmem] * (2 * count),
        out_specs=[in_vmem] * 2,
        out_shape=[
            jax.ShapeDtypeStruct((QUARTERS, half, lags), jnp.float32),
            jax.ShapeDtypeStruct((QUARTERS, half, lags), jnp.bfloat16),
        ],
        compiler_params=pltpu.CompilerParams(vmem_limit_bytes=8 * MIB),
        cost_estimate=pl.CostEstimate(flops=8 * rows * lags, bytes_accessed=32 * rows * lags, transcendentals=0),
    )(place, *kept, *received)


class Grid:
    def __init__(self):
        self.pairs = {}
        side = 4
        for axis in range(2):
            for step in range(1, side):
                moves = []
                for win in range(4):
                    for x in range(side):
                        for y in range(side):
                            for z in range(2):
                                on_x = axis == win % 2
                                nx, ny = ((x + step) % side, y) if on_x else (x, (y + step) % side)
                                moves.append((win * 32 + (x * side + y) * 2 + z, win * 32 + (nx * side + ny) * 2 + z))
                self.pairs[axis, step] = moves

    def move(self, value, axis, step):
        return lax.ppermute(value, ("win", "rcv"), self.pairs[axis, step])

    def flip(self, value):
        return lax.ppermute(value, "rcv", [(i, i ^ 1) for i in range(32)])

    @staticmethod
    def place(index, core):
        x, y = index >> 3, (index >> 1) & 3
        return jnp.where(core == 0, x, y), jnp.where(core == 0, y, x), index & 1


def pick(values, chosen):
    result = values[0]
    for value, this in zip(values[1:], chosen):
        result = jnp.where(this, value, result)
    return result


def at(value, index):
    return lax.dynamic_index_in_dim(value, index, 0, keepdims=False)


def local(spectra, sources, usable, owners):
    windows, parts, channels, bins = spectra.shape
    grid = Grid()
    steps = range(1, QUARTERS)
    owner = owners[0].astype(jnp.int32)
    win = lax.axis_index("win")
    chip, core = win >> 1, win & 1
    rcv = lax.axis_index("rcv")
    u, v, z = grid.place(rcv, core)
    owner_u, owner_v, owner_z = grid.place(owner, core)
    cut_place = jnp.stack([(rcv == owner).astype(jnp.int32), v])
    lag_place = jnp.stack([u, chip])
    end_place = jnp.stack([v, core])
    to_bins = [((u + d) & 3).astype(jnp.uint32) for d in range(QUARTERS)]
    off_v = [(v - owner_v) & 3 == d for d in steps]
    off_u = [(u - owner_u) & 3 == d for d in steps]
    same_z = z == owner_z
    scalars = (cut_place, lag_place, end_place, to_bins, off_v, off_u, same_z)
    scalars, usable = lax.optimization_barrier((scalars, usable))
    cut_place, lag_place, end_place, to_bins, off_v, off_u, same_z = scalars

    flags = jnp.broadcast_to(usable.astype(jnp.float32)[:, :, None], (windows, channels, LANES))
    table = build_table(bins, LAGS, windows * lax.axis_size("win"))
    receiving = mask_receivers(spectra, flags)
    tiles = windows * parts * (bins // LANES)
    cut = cut_sources(sources, flags, cut_place, (1, 2, 3))
    own = cut_sources(sources, flags, cut_place, (0,))
    cut = own + cut
    cut = [part.reshape(QUARTERS, tiles // QUARTERS, ROWS, LANES) for part in cut]
    dealt = [cut[0]] + [grid.move(cut[d], 1, d) for d in steps]
    mine = pick(dealt, off_v)
    mine, table, receiving = lax.optimization_barrier((mine, table, receiving))
    dealt = [at(mine, to_bins[0])] + [grid.move(at(mine, to_bins[d]), 0, d) for d in steps]
    mine = pick(dealt, off_u)
    mine = jnp.where(same_z, mine, grid.flip(mine))
    near = [mine] + [grid.move(mine, 0, d) for d in steps]
    (early,) = lag_quarters(receiving, [mine], table, lag_place, nears=(0,))
    first = jnp.stack(near[:2])
    first_halves = {d: grid.move(first, 1, d) for d in (1, 3)}
    near, early = lax.optimization_barrier((near, early))
    row = jnp.stack(near)
    second = jnp.stack(near[2:])
    quarters = [row, grid.move(second, 1, 1), None, grid.move(second, 1, 3)]

    kept, received = [], []
    for group in GROUPS:
        if group == GROUPS[1]:
            blocks = [first_halves[d].reshape(tiles // 2, ROWS, LANES) for d in group]
            (half,) = lag_quarters(receiving, blocks, table, lag_place, nears=(0, 1))
            row, quarters[1], quarters[3], half = lax.optimization_barrier((row, quarters[1], quarters[3], half))
            quarters[2] = grid.move(row, 1, 2)
            blocks = [quarters[d].reshape(tiles // 2, ROWS, LANES) for d in group]
        else:
            blocks = [quarters[d].reshape(tiles, ROWS, LANES) for d in group]
        if group == GROUPS[0]:
            mine, given = lag_quarters(receiving, blocks, table, lag_place, nears=(1, 2, 3), before=early)
        elif group == GROUPS[1]:
            mine, given = lag_quarters(receiving, blocks, table, lag_place, nears=(2, 3), before=half, held=2)
        elif group != GROUPS[-1]:
            mine, given = lag_quarters(receiving, blocks, table, lag_place)
        else:
            (given,) = lag_quarters(receiving, blocks, table, lag_place, 1)
            given, lag_place = lax.optimization_barrier((given, lag_place))
            (mine,) = lag_quarters(receiving, blocks, table, lag_place, 0)
        mine, lag_place = lax.optimization_barrier((mine, lag_place))
        kept.append(mine)
        received.append(lax.ppermute(given, "win", [(0, 2), (2, 0), (1, 3), (3, 1)]))
    kept, given = split_cores(kept, received, GROUPS, end_place)
    result = kept + lax.ppermute(given, "win", [(0, 1), (1, 0), (2, 3), (3, 2)]).astype(jnp.float32)
    return result.reshape(QUARTERS, 2, channels, LAGS).transpose(1, 0, 2, 3).reshape(2 * QUARTERS, channels, LAGS)


def solution(mesh):
    return jax.shard_map(
        local,
        mesh=mesh,
        in_specs=(P("win", None, "rcv", None), P("win", None, "rcv", None), P("win", "rcv"), P()),
        out_specs=P("win", "rcv", None),
        check_vma=False,
    )
```
